256 devices in a mesh: grp: 8 (over x, core), usr: 32 (over y, z).
Axes of the slice: x: 4, y: 4, z: 8, core: 2. Of those that a mesh axis runs over, the one named last changes fastest.
Arguments:
- candidates: bfloat16 [262144, 1024], P(('grp', 'usr')), may hold values from -6 to 6
- hist_kv: bfloat16 [256, 384, 2048], P(('grp', 'usr')), may hold values from -6 to 6
- hist_len: int32 [256], P(('grp', 'usr')), may hold values from 1 to 384, as said below
- block_mask: int32 [256, 3], P(('grp', 'usr')), may hold values 0 or 1
- tile_user: int32 [4096, 1], P(('grp', 'usr')), may hold values from 0 to 31; in each aligned block of 16 rows (0 to 15, 16 to 31, ...) no two rows name the same one
- tile_count: int32 [4096], P(('grp', 'usr')), may hold values from 1 to 64, as said below
- weight_in: bfloat16 [1024, 4096], P(None, ('grp', 'usr')), may hold values from -0.1875 to 0.1875
- weight_out: bfloat16 [1024, 1024], P(('grp', 'usr')), may hold values from -0.1875 to 0.1875
Outputs:
- scored: bfloat16 [262144, 1024], P(('grp', 'usr'))
The draws below stay inside these ranges and needn't reach their ends.
Inputs may be any that keep to these rules, and one draw needn't show every extreme that they name: `hist_len`: some user's history has exactly 384 items. `tile_count`: the first tile of every device is full. A tile's live candidates take its first slots. `tile_user`: the tiles of one device belong to distinct users of its group.
All inputs are finite; a program needn't handle non-finite values. No bound on the sum of `block_mask` on one device may be relied on, other than what follows from the above.
Results may differ from the reference program's by a relative error of at most 0.0057.
Values may be sent and summed in bfloat16 or wider, within the bound.
No kernel may reach another device: no remote copies, remote signals or barrier semaphores. Data moves between devices by JAX's collectives and lax.ppermute only.
A program may use at most 128 MiB of HBM per device.

```python
import math
import jax
import jax.numpy as jnp
import numpy as np
from jax import lax

D = 1024
HEADS = 8
HIST = 384
BLK = 128
NBLK = 3
TILE = 64
TILES_DEV = 16
USERS = 256
TILES = 4096
CANDS = 262144
N_USR = 32
DEVICES = 256


def draw_hist_len(key, part):
    key = jax.random.fold_in(key, 11)
    lengths = jax.random.randint(key, (USERS,), 1, HIST + 1, dtype=jnp.int32)
    return lengths.at[0].set(HIST)


def draw_tile_count(key, part):
    key = jax.random.fold_in(key, 23)
    counts = jax.random.randint(key, (TILES,), 1, TILE + 1, dtype=jnp.int32)
    first_tile = jnp.arange(TILES, dtype=jnp.int32) % TILES_DEV == 0
    return jnp.where(first_tile, TILE, counts).astype(jnp.int32)


def touch_ends(entries, own_key, least, high):
    shape = entries.shape
    place = [jax.random.randint(jax.random.fold_in(own_key, axis), (), 0, shape[axis]) for axis in range(len(shape))]
    entries = entries.at[tuple(place)].set(least)
    longest = shape.index(max(shape))
    place[longest] = (place[longest] + 1) % shape[longest]
    return entries.at[tuple(place)].set(high)


def levels(key, shape, shards, low, largest):
    loudness = 1.0
    for position, blocks in shards:
        draws = jax.random.uniform(jax.random.fold_in(jax.random.fold_in(key, 6), position), (blocks,), jnp.float32, low / len(shards), largest / len(shards))
        loudness = loudness * jnp.repeat(jnp.exp(draws), shape[position] // blocks).reshape((-1,) + (1,) * (len(shape) - 1 - position))
    return loudness


def deal_out(own_key, own, number, rows, amount, top, most, skew):
    sequence = jax.random.permutation(own_key, amount)
    crowded, ordinary = load_shares(amount, rows * top, most, skew, True), load_shares(amount, rows * top, most, skew, False)
    places = jnp.arange(amount)

    def named(sizes, offset_by):
        used = int((sizes > 0).sum())
        fixed = max(1, used // 4)
        shifted = fixed + (places - fixed + offset_by * (used - fixed)) % max(1, amount - fixed)
        return jnp.zeros((amount,), jnp.int32).at[sequence[jnp.where(places < fixed, places, shifted)]].set(jnp.asarray(sizes, jnp.int32))

    sizes = jnp.where(number % 4 == 0, named(crowded, number // 4), named(ordinary, number - number // 4 - 1))
    mixed = jax.random.permutation(jax.random.fold_in(own, 3), amount)
    source_of, receiver = mixed[0:amount // 2 * 2:2], mixed[1:amount // 2 * 2:2]
    slack = jnp.minimum(sizes[source_of] - 1, most - sizes[receiver]) // 2
    slack = jnp.where((source_of == sequence[0]) | (receiver == sequence[0]) | (sizes[receiver] == 0), 0, jnp.maximum(slack, 0))
    shifted = jax.random.randint(jax.random.fold_in(own, 4), (amount // 2,), 0, 1 << 20) % (slack + 1)
    sizes = sizes.at[source_of].add(-shifted).at[receiver].add(shifted)
    labels = jnp.searchsorted(jnp.cumsum(sizes), jnp.arange(rows * top), side="right").astype(jnp.int32)
    grid = labels.reshape(top, rows).T
    grid = grid[jax.random.permutation(jax.random.fold_in(own, 1), rows)]
    offset_by = jax.random.randint(jax.random.fold_in(own, 2), (rows, 1), 0, top)
    return jnp.take_along_axis(grid, (jnp.arange(top)[None, :] + offset_by) % top, axis=1)


def load_shares(amount, total, most, skew, full):
    weights = [(1 << 20) // math.isqrt(grade ** skew) + 1 for grade in range(1, amount + 1)]
    largest = most if full else min(most, max(-(-total // amount), total * weights[0] // sum(weights)))
    least = 1 if total - largest >= amount - 1 else 0
    holding, surplus = [largest] + [least] * (amount - 1), total - largest - least * (amount - 1)
    while surplus > 0:
        movable = [i for i in range(1, amount) if holding[i] < largest] or [i for i in range(1, amount) if holding[i] < most]
        whole, left = sum([weights[i] for i in movable]), surplus
        for i in movable:
            extra = min(most - holding[i], max(1, left * weights[i] // whole), surplus)
            holding[i] = holding[i] + extra
            surplus = surplus - extra
    return np.array(holding)


def normal_values(rng, shape, deviation, reach, split=(), kind=jnp.bfloat16):
    factor_of = levels(rng, shape, split, -0.22, 0.18) if split else 1.0
    entries = jax.random.normal(rng, shape, jnp.float32) * deviation * factor_of
    return jnp.minimum(jnp.maximum(entries, -reach), reach).astype(kind)


def setup_inputs(seed: int = 0) -> dict:
    key_of = jax.random.split(jax.random.key(seed), 9)
    candidates = normal_values(key_of[0], (CANDS, D), 1.0, 6.0, ((0, 256),))
    hist_kv = normal_values(key_of[1], (USERS, HIST, 2 * D), 1.0, 6.0, ((0, 256),))
    hist_len = draw_hist_len(jax.random.fold_in(key_of[8], 71), 0)
    block_mask = touch_ends((jax.random.randint(key_of[3], (USERS, NBLK), 0, 4) < 3).astype(jnp.int32), jax.random.fold_in(key_of[3], 1), 0, 1)
    tile_user_keys = jax.random.split(jax.random.fold_in(key_of[4], 1), TILES // TILES_DEV)
    tile_user_turns = jax.random.permutation(jax.random.fold_in(key_of[4], 3), TILES // TILES_DEV)
    tile_user = jax.vmap(lambda own, number: deal_out(jax.random.fold_in(key_of[4], 2), own, number, TILES_DEV, N_USR, 1, 1, 2))(tile_user_keys, tile_user_turns).reshape((TILES, 1))
    tile_count = draw_tile_count(jax.random.fold_in(key_of[8], 71), 0)
    weight_in = normal_values(key_of[6], (D, 4 * D), D ** -0.5, 0.1875, ((1, 256),))
    weight_out = normal_values(key_of[7], (D, D), D ** -0.5, 0.1875, ((0, 256),))
    return dict(candidates=candidates, hist_kv=hist_kv, hist_len=hist_len, block_mask=block_mask, tile_user=tile_user, tile_count=tile_count, weight_in=weight_in, weight_out=weight_out)


def norm_rows(values_in):
    centred = values_in - lax.optimization_barrier(jnp.mean(values_in, axis=-1, keepdims=True))
    variance = lax.optimization_barrier(jnp.mean(centred * centred, axis=-1, keepdims=True))
    return centred * lax.rsqrt(variance + 1e-05)

def attend_rows(query_rows, hist_keys, hist_values, live_items, score_scale):
    row_total = query_rows.shape[0]
    model_width = query_rows.shape[1]
    head_dim = model_width // HEADS
    query_heads = query_rows.astype(jnp.float32).reshape(row_total, HEADS, head_dim)
    key_heads = hist_keys.astype(jnp.float32).reshape(-1, HEADS, head_dim)
    value_heads = hist_values.astype(jnp.float32).reshape(-1, HEADS, head_dim)
    scores = jnp.einsum('nhd,lhd->hnl', query_heads, key_heads) * score_scale
    weights = (jax.nn.silu(scores) * live_items).astype(jnp.bfloat16)
    attended = jnp.einsum('hnl,lhd->nhd', weights.astype(jnp.float32), value_heads)
    return attended.reshape(row_total, model_width)

def own_term(queries, self_keys, self_values, score_scale):
    row_total = queries.shape[0]
    products = (queries.astype(jnp.float32) * self_keys.astype(jnp.float32)).reshape(row_total, HEADS, -1)
    strength = jax.nn.silu(lax.optimization_barrier(jnp.sum(products, axis=2)) * score_scale)
    value_heads = self_values.astype(jnp.float32).reshape(row_total, HEADS, -1)
    return (strength[:, :, None] * value_heads).reshape(row_total, -1)

def reference(candidates, hist_kv, hist_len, block_mask, tile_user, tile_count, weight_in, weight_out):
    score_scale = (D // HEADS) ** (-0.5)
    positions = jnp.arange(HIST, dtype=jnp.int32)
    device_ids = jnp.arange(DEVICES, dtype=jnp.int32)
    group_base = device_ids // N_USR * N_USR
    rows_dev = candidates.reshape(DEVICES, TILES_DEV * TILE, D)
    users_dev = tile_user.reshape(DEVICES, TILES_DEV).astype(jnp.int32) + group_base[:, None]
    counts_dev = tile_count.reshape(DEVICES, TILES_DEV)

    def one_device(packed):
        cand_rows, tile_users, tile_counts = packed
        normed = norm_rows(cand_rows.astype(jnp.float32)).astype(jnp.bfloat16)
        projected = jax.nn.silu(jnp.dot(normed, weight_in, preferred_element_type=jnp.float32)).astype(jnp.bfloat16)
        queries = projected[:, :D]
        self_keys = projected[:, D:2 * D]
        self_values = projected[:, 2 * D:3 * D]
        gate_units = projected[:, 3 * D:]
        own_part = own_term(queries, self_keys, self_values, score_scale)

        def one_tile(packed_tile):
            tile_queries, user_id = packed_tile
            user_cache = lax.dynamic_index_in_dim(hist_kv, user_id, 0, keepdims=False)
            length = lax.dynamic_index_in_dim(hist_len, user_id, 0, keepdims=False)
            user_blocks = lax.dynamic_index_in_dim(block_mask, user_id, 0, keepdims=False)
            live_items = ((positions < length) & (jnp.repeat(user_blocks, BLK) > 0)).astype(jnp.float32)
            return attend_rows(tile_queries, user_cache[:, :D], user_cache[:, D:], live_items, score_scale).astype(jnp.bfloat16)
        history = lax.map(one_tile, (queries.reshape(TILES_DEV, TILE, D), tile_users)).reshape(TILES_DEV * TILE, D)
        combined = history.astype(jnp.float32) + own_part
        gated_rows = (norm_rows(combined) * gate_units.astype(jnp.float32)).astype(jnp.bfloat16)
        mixed_rows = jnp.dot(gated_rows, weight_out, preferred_element_type=jnp.float32) + cand_rows.astype(jnp.float32)
        live_rows = (jnp.arange(TILE, dtype=jnp.int32)[None, :] < tile_counts[:, None]).reshape(-1)
        return jnp.where(live_rows[:, None], mixed_rows, 0.0).astype(jnp.bfloat16)
    scored = lax.map(one_device, (rows_dev, users_dev, counts_dev))
    return scored.reshape(TILES * TILE, D)
```

```python
import functools

import jax
import jax.numpy as jnp
from jax import lax
from jax.experimental import pallas as pl
from jax.experimental.pallas import tpu as pltpu
from jax.sharding import Mesh
from jax.sharding import PartitionSpec as P

HEADS = 8
HEAD = 128
BLK = 128
HIST = 384
TILE = 64
ROWS = 256
CHUNKS = 2
META = 4
NX, NC, NY, NZ = 4, 2, 4, 8
BF = jnp.bfloat16
F32 = jnp.float32
VMEM_LIMIT = 56 * 1024 * 1024
NT = (((1,), (1,)), ((), ()))


def half_silu(a):
    return a + a * jnp.tanh(a)


def params():
    return pltpu.CompilerParams(vmem_limit_bytes=VMEM_LIMIT)


def ring(size, step):
    return [(i, (i + step) % size) for i in range(size)]


def prep_kernel(len_ref, mask_ref, key_in, value_in, key_out, value_out):
    place = lax.broadcasted_iota(jnp.int32, (HIST, HEAD), 0)
    kept = jnp.where(
        place < BLK, mask_ref[0, 0], jnp.where(place < 2 * BLK, mask_ref[0, 1], mask_ref[0, 2])
    )
    live = (place < len_ref[0]) & (kept > 0)
    key_out[0] = key_in[...]
    value_out[0] = jnp.where(live, value_in[...].astype(F32), 0.0).astype(BF)


def prep(hist, hist_len, block_mask):
    shape = jax.ShapeDtypeStruct((HEADS, HIST, HEAD), BF)
    smem = pl.BlockSpec(memory_space=pltpu.SMEM)
    return pl.pallas_call(
        prep_kernel,
        grid=(HEADS,),
        in_specs=[
            smem,
            smem,
            pl.BlockSpec((HIST, HEAD), lambda h: (0, h)),
            pl.BlockSpec((HIST, HEAD), lambda h: (0, HEADS + h)),
        ],
        out_specs=[pl.BlockSpec((1, HIST, HEAD), lambda h: (h, 0, 0))] * 2,
        out_shape=[shape, shape],
        compiler_params=params(),
        name="prep",
    )(hist_len, block_mask, hist, hist)


def norm_kernel(rows_ref, out_ref):
    values = rows_ref[...].astype(F32)
    centred = values - jnp.mean(values, axis=-1, keepdims=True)
    variance = jnp.mean(centred * centred, axis=-1, keepdims=True)
    out_ref[...] = (centred * lax.rsqrt(variance + 1e-05)).astype(BF)


def norm(rows):
    total, width = rows.shape
    return pl.pallas_call(
        norm_kernel,
        grid=(total // ROWS,),
        in_specs=[pl.BlockSpec((ROWS, width), lambda i: (i, 0))],
        out_specs=pl.BlockSpec((ROWS, width), lambda i: (i, 0)),
        out_shape=jax.ShapeDtypeStruct((total, width), BF),
        compiler_params=params(),
        name="norm",
    )(rows)


def query_kernel(slot_ref, rows_ref, mine_ref, other_ref, out_ref):
    rows = rows_ref[...]
    for part, weights in enumerate((mine_ref, other_ref)):
        for pair in range(2):
            block = weights[pl.ds(pair * 2 * HEAD, 2 * HEAD), :]
            made = lax.dot_general(rows, block, NT, preferred_element_type=F32)
            made = half_silu(made * 0.5).astype(BF)
            for lane in range(2):
                slot = slot_ref[part * 4 + pair * 2 + lane]
                out_ref[slot] = made[:, lane * HEAD : (lane + 1) * HEAD]


def query(slots, normed, mine, other, chunk):
    width = normed.shape[1]
    rows = normed.shape[0] // CHUNKS
    steps = rows // ROWS
    half = pl.BlockSpec((4 * HEAD, width), lambda i: (0, 0))
    return pl.pallas_call(
        query_kernel,
        grid=(steps,),
        in_specs=[
            pl.BlockSpec(memory_space=pltpu.SMEM),
            pl.BlockSpec((ROWS, width), lambda i: (chunk * steps + i, 0)),
            half,
            half,
        ],
        out_specs=pl.BlockSpec((HEADS, ROWS, HEAD), lambda i: (0, i, 0)),
        out_shape=jax.ShapeDtypeStruct((HEADS, rows, HEAD), BF),
        compiler_params=params(),
        name="query",
    )(slots, normed, mine, other)


def attend_kernel(scale, user_ref, query_ref, key_ref, value_ref, out_ref):
    source = pl.program_id(0)
    tiles = query_ref.shape[1] // TILE
    for t in range(tiles):
        user = user_ref[source, t]
        scores = lax.dot_general(
            query_ref[0, pl.ds(t * TILE, TILE), :], key_ref[user], NT, preferred_element_type=F32
        )
        weights = half_silu(scores * (0.5 * scale)).astype(BF)
        out_ref[0, pl.ds(t * TILE, TILE), :] = jnp.dot(
            weights, value_ref[user], preferred_element_type=F32
        ).astype(BF)


def attend(users, queries, keys, values, scale):
    count, rows, _ = queries.shape
    whole = pl.BlockSpec(keys.shape, lambda i: (0, 0, 0))
    return pl.pallas_call(
        functools.partial(attend_kernel, scale),
        grid=(count,),
        in_specs=[
            pl.BlockSpec(memory_space=pltpu.SMEM),
            pl.BlockSpec((1, rows, HEAD), lambda i: (i, 0, 0)),
            whole,
            whole,
        ],
        out_specs=pl.BlockSpec((1, rows, HEAD), lambda i: (i, 0, 0)),
        out_shape=jax.ShapeDtypeStruct(queries.shape, BF),
        compiler_params=params(),
        name="attend",
    )(users, queries, keys, values)


def own_kernel(scale, rows_ref, query_ref, key_w, value_w, gate_w, own_ref, gate_ref):
    rows = rows_ref[...]
    width = rows.shape[1]

    def project(weights, start):
        block = weights[pl.ds(start // HEAD, 2)].reshape(2 * HEAD, width)
        made = lax.dot_general(rows, block, NT, preferred_element_type=F32)
        return half_silu(made * 0.5).astype(BF)

    for start in range(0, width, 2 * HEAD):
        self_keys = project(key_w, start).astype(F32)
        self_values = project(value_w, start).astype(F32)
        gate_ref[:, start : start + 2 * HEAD] = project(gate_w, start)
        for lane in range(2):
            cut = slice(lane * HEAD, (lane + 1) * HEAD)
            head = start // HEAD + lane
            products = query_ref[head].astype(F32) * self_keys[:, cut]
            strength = half_silu(jnp.sum(products, axis=1, keepdims=True) * (0.5 * scale))
            own_ref[:, head * HEAD : (head + 1) * HEAD] = strength * self_values[:, cut]


def own(normed, queries, gathered, chunk, scale):
    width = normed.shape[1]
    rows = queries.shape[1]
    steps = rows // ROWS

    def weights(place):
        return pl.BlockSpec((HEADS, HEAD, width), lambda i: (place, 0, 0))

    return pl.pallas_call(
        functools.partial(own_kernel, scale),
        grid=(steps,),
        in_specs=[
            pl.BlockSpec((ROWS, width), lambda i: (chunk * steps + i, 0)),
            pl.BlockSpec((HEADS, ROWS, HEAD), lambda i: (0, i, 0)),
            weights(1),
            weights(2),
            weights(3),
        ],
        out_specs=[pl.BlockSpec((ROWS, width), lambda i: (i, 0))] * 2,
        out_shape=[
            jax.ShapeDtypeStruct((rows, width), F32),
            jax.ShapeDtypeStruct((rows, width), BF),
        ],
        compiler_params=params(),
        name="own",
    )(normed, queries, gathered, gathered, gathered)


def finish_kernel(chunk, count_ref, hist_ref, own_ref, gate_ref, out_w, rows_ref, *rest):
    out_ref = rest[-1]
    width = rows_ref.shape[1]
    history = jnp.concatenate([hist_ref[h].astype(F32) for h in range(HEADS)], axis=1)
    combined = history + own_ref[...]
    centred = combined - jnp.mean(combined, axis=-1, keepdims=True)
    variance = jnp.mean(centred * centred, axis=-1, keepdims=True)
    gated = (centred * lax.rsqrt(variance + 1e-05) * gate_ref[...].astype(F32)).astype(BF)
    weights = out_w[...].reshape(width, width)
    mixed = jnp.dot(gated, weights, preferred_element_type=F32) + rows_ref[...].astype(F32)
    first = (chunk * pl.num_programs(0) + pl.program_id(0)) * (ROWS // TILE)
    slot = lax.broadcasted_iota(jnp.int32, (TILE, width), 0)
    for t in range(ROWS // TILE):
        cut = slice(t * TILE, (t + 1) * TILE)
        out_ref[cut, :] = jnp.where(slot < count_ref[first + t], mixed[cut, :], 0.0).astype(BF)


def finish(counts, history, own_part, gate, gathered, rows, chunk, before):
    total, width = rows.shape
    steps = total // CHUNKS // ROWS
    place = pl.BlockSpec((ROWS, width), lambda i: (chunk * steps + i, 0))
    local = pl.BlockSpec((ROWS, width), lambda i: (i, 0))
    shares = gathered.shape[0]
    out_rows = width // shares
    specs = [
        pl.BlockSpec(memory_space=pltpu.SMEM),
        pl.BlockSpec((HEADS, ROWS, HEAD), lambda i: (0, i, 0)),
        local,
        local,
        pl.BlockSpec((shares, out_rows, width), lambda i: (0, HEAD // out_rows, 0)),
        place,
    ]
    given = [counts, history, own_part, gate, gathered, rows]
    aliases = {}
    if before is not None:
        specs.append(pl.BlockSpec(memory_space=pl.ANY))
        given.append(before)
        aliases = {len(given) - 1: 0}
    return pl.pallas_call(
        functools.partial(finish_kernel, chunk),
        grid=(steps,),
        in_specs=specs,
        out_specs=place,
        out_shape=jax.ShapeDtypeStruct((total, width), BF),
        input_output_aliases=aliases,
        compiler_params=params(),
        name="finish",
    )(*given)


def swap_z(values):
    return lax.all_to_all(values, "z", split_axis=0, concat_axis=0, tiled=True)


def shards(candidates, hist_kv, hist_len, block_mask, tile_user, tile_count, weight_in, weight_out):
    width = candidates.shape[1]
    tiles = tile_user.shape[0]
    scale = HEAD ** (-0.5)
    at_x, at_core, at_y = lax.axis_index("x"), lax.axis_index("core"), lax.axis_index("y")

    columns = weight_in.T
    share = columns.shape[0]
    sent = [lax.ppermute(columns, "x", [(0, k)]) for k in range(1, NX)]
    query_part = jnp.where(at_x == 0, columns, sent[0] + sent[1] + sent[2])
    query_z = swap_z(jnp.broadcast_to(query_part, (NZ, share, width)))

    meta = jnp.zeros((META, width), BF).at[0, :tiles].set(tile_user[:, 0].astype(BF))
    packed = jnp.concatenate([columns, weight_out, meta], axis=0)
    packed, query_part = lax.optimization_barrier((packed, query_part))
    rest_z = swap_z(jnp.broadcast_to(packed, (NZ,) + packed.shape))
    users = rest_z[:, share + weight_out.shape[0], :tiles].astype(jnp.int32)

    keys, values = prep(hist_kv[0], hist_len, block_mask)
    keys = swap_z(keys)
    values = swap_z(values)

    query_z = query_z.reshape(NZ * share, width)
    query_y = [query_z]
    for step in range(1, NY):
        query_y.append(lax.ppermute(query_z, "y", ring(NY, step)))
    mine = jnp.concatenate(query_y, axis=0)
    other = lax.ppermute(mine, "core", ring(NC, 1))
    at = (at_y - jnp.arange(NY, dtype=jnp.int32)) % NY
    slots = jnp.concatenate([at_core * NY + at, (1 - at_core) * NY + at]).astype(jnp.int32)

    in_rows = rest_z[:, :share].reshape(NZ * share, width)
    out_rows = rest_z[:, share : share + weight_out.shape[0]].reshape(-1, width)
    gathered = lax.all_gather(jnp.concatenate([in_rows, out_rows], axis=0), ("x", "core", "y"))

    key_up = lax.ppermute(keys, "y", ring(NY, 1))
    key_down = lax.ppermute(keys, "y", ring(NY, NY - 1))
    value_up = lax.ppermute(values, "y", ring(NY, 1))
    value_down = lax.ppermute(values, "y", ring(NY, NY - 1))
    key_far = lax.ppermute(key_up, "y", ring(NY, 1))
    value_far = lax.ppermute(value_down, "y", ring(NY, NY - 1))
    all_keys = jnp.concatenate([keys, key_up, key_far, key_down], axis=0)
    all_values = jnp.concatenate([values, value_up, value_far, value_down], axis=0)
    users = ((at_y - users // NZ) % NY) * NZ + users % NZ

    normed = norm(candidates)
    queries = [query(slots, normed, mine, other, c) for c in range(CHUNKS)]
    arrived = [swap_z(q) for q in queries]
    per = tiles // CHUNKS
    history = []
    for c in range(CHUNKS):
        part = users[:, c * per : (c + 1) * per]
        history.append(swap_z(attend(part, arrived[c], all_keys, all_values, scale)))
    out = None
    for c in range(CHUNKS):
        own_part, gate = own(normed, queries[c], gathered, c, scale)
        out = finish(tile_count, history[c], own_part, gate, gathered, candidates, c, out)
    return out


def solution(mesh):
    fine = Mesh(mesh.devices.reshape(NX, NC, NY, NZ), ("x", "core", "y", "z"))
    every = ("x", "core", "y", "z")
    in_specs = (
        P(every, None),
        P(every, None, None),
        P(every),
        P(every, None),
        P(every, None),
        P(every),
        P(None, every),
        P(every, None),
    )
    return jax.shard_map(
        shards, mesh=fine, in_specs=in_specs, out_specs=P(every, None), check_vma=False
    )
```

```python
import functools

import jax
import jax.numpy as jnp
from jax import lax
from jax.experimental import pallas as pl
from jax.experimental.pallas import tpu as pltpu
from jax.sharding import Mesh
from jax.sharding import PartitionSpec as P

HEADS = 8
HEAD = 128
BLK = 128
HIST = 384
TILE = 64
CHUNKS = 2
META = 4
SPARE = 16
NX, NC, NY, NZ = 4, 2, 4, 8
BF = jnp.bfloat16
F32 = jnp.float32
MIB = 1024 * 1024
SIZES = (768, 832, 1024)
NT = (((1,), (1,)), ((), ()))


def half_silu(a):
    return a + a * jnp.tanh(a)


def params(limit=16):
    return pltpu.CompilerParams(vmem_limit_bytes=limit * MIB)


def ring(size, step):
    return [(i, (i + step) % size) for i in range(size)]


def prep_kernel(len_ref, mask_ref, hist_ref, out_ref):
    place = lax.broadcasted_iota(jnp.int32, (HIST, HEAD), 0)
    kept = jnp.where(
        place < BLK, mask_ref[0, 0], jnp.where(place < 2 * BLK, mask_ref[0, 1], mask_ref[0, 2])
    )
    live = (place < len_ref[0]) & (kept > 0)
    width = HEADS * HEAD
    for h in range(HEADS):
        cut = slice(h * HEAD, (h + 1) * HEAD)
        out_ref[h, :HIST, :] = hist_ref[:, cut]
        values = hist_ref[:, width + h * HEAD : width + (h + 1) * HEAD].astype(F32)
        out_ref[h, HIST:, :] = jnp.where(live, values, 0.0).astype(BF)


def prep(hist, hist_len, block_mask):
    smem = pl.BlockSpec(memory_space=pltpu.SMEM)
    vmem = pl.BlockSpec(memory_space=pltpu.VMEM)
    return pl.pallas_call(
        prep_kernel,
        in_specs=[smem, smem, vmem],
        out_specs=vmem,
        out_shape=jax.ShapeDtypeStruct((HEADS, 2 * HIST, HEAD), BF),
        compiler_params=params(),
        name="prep",
    )(hist_len, block_mask, hist)


def norm_kernel(place_ref, rows_ref, out_ref, packed):
    total = rows_ref.shape[0]
    packed[...] = jnp.zeros_like(packed)
    for t in range(total // TILE):
        values = rows_ref[t * TILE : (t + 1) * TILE, :].astype(F32)
        centred = values - jnp.mean(values, axis=-1, keepdims=True)
        variance = jnp.mean(centred * centred, axis=-1, keepdims=True)
        normed = centred * lax.rsqrt(variance + 1e-05)
        for h in range(HEADS):
            packed[h, pl.ds(place_ref[t], TILE), :] = normed[:, h * HEAD : (h + 1) * HEAD]
    for h in range(HEADS):
        out_ref[:, h * HEAD : (h + 1) * HEAD] = packed[h, :total, :].astype(BF)


def norm(places, rows):
    total, width = rows.shape
    vmem = pl.BlockSpec(memory_space=pltpu.VMEM)
    return pl.pallas_call(
        norm_kernel,
        in_specs=[pl.BlockSpec(memory_space=pltpu.SMEM), vmem],
        out_specs=vmem,
        out_shape=jax.ShapeDtypeStruct((total, width), BF),
        scratch_shapes=[pltpu.VMEM((HEADS, total + TILE, HEAD), F32)],
        compiler_params=params(),
        name="norm",
    )(places, rows)


def query_kernel(start, slot_ref, rows_ref, mine_ref, other_ref, out_ref):
    rows = rows_ref[start : start + out_ref.shape[1], :]
    share = mine_ref.shape[0] // NY
    for part, weights in enumerate((mine_ref, other_ref)):
        for pair in range(2):
            block = jnp.concatenate(
                [weights[(2 * pair + k) * share : (2 * pair + k) * share + HEAD, :] for k in range(2)]
            )
            made = lax.dot_general(rows, block, NT, preferred_element_type=F32)
            made = half_silu(made * 0.5).astype(BF)
            for lane in range(2):
                slot = slot_ref[part * 4 + pair * 2 + lane]
                out_ref[slot] = made[:, lane * HEAD : (lane + 1) * HEAD]


def query(slots, normed, mine, other, rows, chunk):
    vmem = pl.BlockSpec(memory_space=pltpu.VMEM)
    return pl.pallas_call(
        functools.partial(query_kernel, rows * chunk),
        in_specs=[pl.BlockSpec(memory_space=pltpu.SMEM), vmem, vmem, vmem],
        out_specs=vmem,
        out_shape=jax.ShapeDtypeStruct((HEADS, rows, HEAD), BF),
        compiler_params=params(),
        name="query",
    )(slots, normed, mine, other)


def attend_kernel(scale, base, user_ref, place_ref, span_ref, query_ref, cache_ref, out_ref, held, made):
    sources, rows, _ = query_ref.shape
    held[:, :rows, :] = query_ref[...].astype(F32)
    held[:, rows:, :] = jnp.zeros((sources, TILE, HEAD), F32)

    def step(j, carry):
        tiles = [jnp.minimum(span_ref[s, 0] + j, span_ref[s, 1]) for s in range(sources)]
        users = [user_ref[s, t] for s, t in enumerate(tiles)]
        starts = [jnp.clip(place_ref[s, t] - base, 0, rows) for s, t in enumerate(tiles)]
        scores = [
            lax.dot_general(
                held[s, pl.ds(start, TILE), :].astype(BF),
                cache_ref[u, :HIST, :],
                NT,
                preferred_element_type=F32,
            )
            for s, (u, start) in enumerate(zip(users, starts))
        ]
        weights = [half_silu(score * (0.5 * scale)).astype(BF) for score in scores]
        for s, (u, start) in enumerate(zip(users, starts)):
            made[s, pl.ds(start, TILE), :] = jnp.dot(
                weights[s], cache_ref[u, HIST:, :], preferred_element_type=F32
            )
        return carry

    lax.fori_loop(0, span_ref[0, 2], step, 0)
    out_ref[...] = made[:, :rows, :].astype(BF)


def attend(users, places, counts, queries, caches, chunk, scale):
    sources, rows, _ = queries.shape
    base = rows * chunk
    first = jnp.sum(places + counts <= base, axis=1)
    last = jnp.sum(places < base + rows, axis=1) - 1
    top = users.shape[1] - 1
    first, last = jnp.clip(first, 0, top), jnp.clip(last, 0, top)
    last = jnp.maximum(first, last)
    trips = jnp.broadcast_to(jnp.max(last - first) + 1, first.shape)
    spans = jnp.stack([first, last, trips], axis=1).astype(jnp.int32)
    vmem = pl.BlockSpec(memory_space=pltpu.VMEM)
    smem = pl.BlockSpec(memory_space=pltpu.SMEM)
    return pl.pallas_call(
        functools.partial(attend_kernel, scale, base),
        in_specs=[smem, smem, smem, vmem, vmem],
        out_specs=vmem,
        out_shape=jax.ShapeDtypeStruct(queries.shape, BF),
        scratch_shapes=[pltpu.VMEM((sources, rows + TILE, HEAD), F32)] * 2,
        compiler_params=params(),
        name="attend",
    )(users, places, spans, queries, caches)


def own_kernel(scale, start, rows_ref, query_ref, gathered, own_ref, gate_ref, *out_w):
    rows = rows_ref[start : start + query_ref.shape[1], :]
    width = rows.shape[1]

    def project(place, column):
        first = HEADS * place + column // HEAD
        block = gathered[first : first + 2, :HEAD, :].reshape(2 * HEAD, width)
        made = lax.dot_general(rows, block, NT, preferred_element_type=F32)
        return half_silu(made * 0.5).astype(BF)

    for column in range(0, width, 2 * HEAD):
        self_keys = project(1, column).astype(F32)
        self_values = project(2, column).astype(F32)
        gate_ref[:, column : column + 2 * HEAD] = project(3, column)
        for lane in range(2):
            cut = slice(lane * HEAD, (lane + 1) * HEAD)
            head = column // HEAD + lane
            products = query_ref[head].astype(F32) * self_keys[:, cut]
            strength = half_silu(jnp.sum(products, axis=1, keepdims=True) * (0.5 * scale))
            own_ref[:, head * HEAD : (head + 1) * HEAD] = strength * self_values[:, cut]
    for out in out_w:
        out[...] = gathered[:, HEAD:, :].reshape(width, width)


def own(normed, queries, gathered, chunk, scale):
    width = normed.shape[1]
    rows = queries.shape[1]
    vmem = pl.BlockSpec(memory_space=pltpu.VMEM)
    shapes = [((rows, width), F32), ((rows, width), BF)] + [((width, width), BF)] * (chunk == 0)
    return pl.pallas_call(
        functools.partial(own_kernel, scale, rows * chunk),
        in_specs=[vmem] * 3,
        out_specs=[vmem] * len(shapes),
        out_shape=[jax.ShapeDtypeStruct(shape, kind) for shape, kind in shapes],
        compiler_params=params(),
        name="own",
    )(normed, queries, gathered)


def mix(hist_ref, own_ref, gate_ref, out_w, cut):
    history = jnp.concatenate([hist_ref[h, cut, :].astype(F32) for h in range(HEADS)], axis=1)
    combined = history + own_ref[cut, :]
    centred = combined - jnp.mean(combined, axis=-1, keepdims=True)
    variance = jnp.mean(centred * centred, axis=-1, keepdims=True)
    gated = centred * lax.rsqrt(variance + 1e-05) * gate_ref[cut, :].astype(F32)
    return jnp.dot(gated.astype(BF), out_w[...], preferred_element_type=F32)


def pieces(rows):
    step = 128 if rows % 128 == 0 else rows // 2
    return [slice(start, start + step) for start in range(0, rows, step)]


def first_kernel(hist_ref, own_ref, gate_ref, out_w, out_ref):
    for cut in pieces(own_ref.shape[0]):
        out_ref[cut, :] = mix(hist_ref, own_ref, gate_ref, out_w, cut)


def last_kernel(count_ref, place_ref, hist_ref, own_ref, gate_ref, out_w, before, rows_ref, out_ref, mixed):
    rows, width = own_ref.shape
    heads = [slice(h * HEAD, (h + 1) * HEAD) for h in range(HEADS)]
    mixed[:, 2 * rows :, :] = jnp.zeros((HEADS, TILE, HEAD), F32)
    for h, columns in enumerate(heads):
        mixed[h, :rows, :] = before[:, columns]
    for cut in pieces(rows):
        made = mix(hist_ref, own_ref, gate_ref, out_w, cut)
        for h, columns in enumerate(heads):
            mixed[h, rows + cut.start : rows + cut.stop, :] = made[:, columns]
    slot = lax.broadcasted_iota(jnp.int32, (TILE, HEAD), 0)
    for t in range(rows_ref.shape[0] // TILE):
        cut = slice(t * TILE, (t + 1) * TILE)
        live = slot < count_ref[t]
        for h, columns in enumerate(heads):
            scored = mixed[h, pl.ds(place_ref[t], TILE), :] + rows_ref[cut, columns].astype(F32)
            out_ref[cut, columns] = jnp.where(live, scored, 0.0).astype(BF)


def finish(counts, places, history, own_parts, gates, out_w, candidates):
    rows, width = own_parts[0].shape
    vmem = pl.BlockSpec(memory_space=pltpu.VMEM)
    smem = pl.BlockSpec(memory_space=pltpu.SMEM)
    before = pl.pallas_call(
        first_kernel,
        in_specs=[vmem] * 4,
        out_specs=vmem,
        out_shape=jax.ShapeDtypeStruct((rows, width), F32),
        compiler_params=params(),
        name="first",
    )(history[0], own_parts[0], gates[0], out_w)
    return pl.pallas_call(
        last_kernel,
        in_specs=[smem, smem] + [vmem] * 6,
        out_specs=vmem,
        out_shape=jax.ShapeDtypeStruct(candidates.shape, BF),
        scratch_shapes=[pltpu.VMEM((HEADS, 2 * rows + TILE, HEAD), F32)],
        compiler_params=params(),
        name="last",
    )(counts, places, history[1], own_parts[1], gates[1], out_w, before, candidates)


def swap_z(values):
    return lax.all_to_all(values, "z", split_axis=0, concat_axis=0, tiled=True)


def after(scale, size, normed, mine, other, slots, caches, rest, users, places, counts, mine_places, mine_counts, candidates):
    rows = size // CHUNKS
    gathered = lax.all_gather(rest, ("x", "core", "y"))
    queries = [query(slots, normed, mine, other, rows, c) for c in range(CHUNKS)]
    arrived = [swap_z(q) for q in queries]
    up = lax.ppermute(caches, "y", ring(NY, 1))
    down = lax.ppermute(caches, "y", ring(NY, NY - 1))
    far = [
        lax.ppermute(up[:, :HIST], "y", ring(NY, 1)),
        lax.ppermute(down[:, HIST:], "y", ring(NY, NY - 1)),
    ]
    caches = jnp.concatenate([caches, up, jnp.concatenate(far, axis=1), down], axis=0)
    history, own_parts, gates = [], [], []
    out_w = None
    for c in range(CHUNKS):
        made = attend(users, places, counts, arrived[c], caches, c, scale)
        history.append(swap_z(made))
        parts = own(normed, queries[c], gathered, c, scale)
        own_parts.append(parts[0])
        gates.append(parts[1])
        out_w = parts[2] if c == 0 else out_w
    return finish(mine_counts, mine_places, history, own_parts, gates, out_w, candidates)


def shards(candidates, hist_kv, hist_len, block_mask, tile_user, tile_count, weight_in, weight_out):
    width = candidates.shape[1]
    tiles = tile_user.shape[0]
    scale = HEAD ** (-0.5)
    at_x, at_core, at_y = [lax.axis_index(name) for name in ("x", "core", "y")]

    ends = jnp.cumsum(tile_count)
    mine_places = (ends - tile_count).astype(jnp.int32)
    grade = sum([(ends[-1] > size).astype(jnp.int32) for size in SIZES[:-1]])

    columns = weight_in.T
    share, out_share = columns.shape[0], weight_out.shape[0]
    cut = prep(hist_kv[0], hist_len, block_mask)
    normed = norm(mine_places, candidates)

    told = jnp.full((SPARE, width), grade, jnp.int32).astype(BF)
    named = jnp.concatenate([columns, told], axis=0)
    sent = [named] + [lax.ppermute(named, "x", ring(NX, k)) for k in range(1, NX)]
    query_part = sent[0][:share]
    for k in range(1, NX):
        query_part = jnp.where(at_x == k, sent[k][:share], query_part)
        told = jnp.maximum(told, sent[k][share:])
    meta = jnp.zeros((META, width), BF).at[0, :tiles].set(tile_user[:, 0].astype(BF))
    meta = meta.at[1, :tiles].set(tile_count.astype(BF)).at[2].set(told[0])
    packed = jnp.concatenate([query_part, columns, weight_out, meta], axis=0)
    packed, cut, normed = lax.optimization_barrier((packed, cut, normed))
    spread = swap_z(jnp.broadcast_to(packed, (NZ,) + packed.shape))
    spread, cut = lax.optimization_barrier((spread, cut))
    caches = swap_z(cut)
    query_z = spread[:, :share].reshape(NZ * share, width)
    in_rows = spread[:, share : 2 * share].reshape(NZ * share, width)
    out_rows = spread[:, 2 * share : 2 * share + out_share].reshape(NZ * out_share, width)
    rest = jnp.concatenate([in_rows, out_rows], axis=0)
    meta = spread[:, 2 * share + out_share :]
    users = meta[:, 0, :tiles].astype(jnp.int32)
    counts = meta[:, 1, :tiles].astype(jnp.int32)
    places = jnp.cumsum(counts, axis=1) - counts
    users = ((at_y - users // NZ) % NY) * NZ + users % NZ
    told = jnp.broadcast_to(jnp.max(meta[:, 2], axis=0), (SPARE, width))

    query_z = jnp.concatenate([query_z, told], axis=0)
    query_y = [query_z]
    for step in range(1, NY):
        query_y.append(lax.ppermute(query_z, "y", ring(NY, step)))
    mine = jnp.concatenate(query_y, axis=0)
    other = lax.ppermute(mine, "core", ring(NC, 1))
    at = (at_y - jnp.arange(NY, dtype=jnp.int32)) % NY
    slots = jnp.concatenate([at_core * NY + at, (1 - at_core) * NY + at]).astype(jnp.int32)
    heard = jnp.stack([mine, other]).reshape(NC * NY, -1, width)[:, NZ * share, 0]
    choice = jnp.max(heard).astype(jnp.int32)

    given = (normed, mine, other, slots, caches, rest, users, places, counts)
    given = given + (mine_places, tile_count, candidates)
    return lax.switch(choice, [functools.partial(after, scale, size) for size in SIZES], *given)


def solution(mesh):
    fine = Mesh(mesh.devices.reshape(NX, NC, NY, NZ), ("x", "core", "y", "z"))
    every = ("x", "core", "y", "z")
    in_specs = (
        P(every, None),
        P(every, None, None),
        P(every),
        P(every, None),
        P(every, None),
        P(every),
        P(None, every),
        P(every, None),
    )
    return jax.shard_map(
        shards, mesh=fine, in_specs=in_specs, out_specs=P(every, None), check_vma=False
    )
```

```python
import functools

import jax
import jax.numpy as jnp
from jax import lax
from jax.experimental import pallas as pl
from jax.experimental.pallas import tpu as pltpu
from jax.sharding import Mesh
from jax.sharding import PartitionSpec as P

HEADS = 8
HEAD = 128
BLK = 128
HIST = 384
TILE = 64
CHUNKS = 2
META = 8
PIECE = 128
NX, NC, NY, NZ = 4, 2, 4, 8
BF = jnp.bfloat16
F32 = jnp.float32
MIB = 1024 * 1024
NT = (((1,), (1,)), ((), ()))


def half_silu(a):
    return a + a * jnp.tanh(a)


def params(limit=16):
    return pltpu.CompilerParams(vmem_limit_bytes=limit * MIB)


def ring(size, step):
    return [(i, (i + step) % size) for i in range(size)]


def prep_kernel(len_ref, mask_ref, hist_ref, out_ref):
    place = lax.broadcasted_iota(jnp.int32, (HIST, HEAD), 0)
    kept = jnp.where(
        place < BLK, mask_ref[0, 0], jnp.where(place < 2 * BLK, mask_ref[0, 1], mask_ref[0, 2])
    )
    live = (place < len_ref[0]) & (kept > 0)
    width = HEADS * HEAD
    for h in range(HEADS):
        cut = slice(h * HEAD, (h + 1) * HEAD)
        for b in range(0, HIST, BLK):
            turned = hist_ref[b : b + BLK, cut].astype(F32).T
            out_ref[h, b : b + BLK, :] = turned.astype(BF)
        values = hist_ref[:, width + h * HEAD : width + (h + 1) * HEAD].astype(F32)
        out_ref[h, HIST:, :] = jnp.where(live, values, 0.0).astype(BF)


def prep(hist, hist_len, block_mask):
    smem = pl.BlockSpec(memory_space=pltpu.SMEM)
    vmem = pl.BlockSpec(memory_space=pltpu.VMEM)
    return pl.pallas_call(
        prep_kernel,
        in_specs=[smem, smem, vmem],
        out_specs=vmem,
        out_shape=jax.ShapeDtypeStruct((HEADS, 2 * HIST, HEAD), BF),
        compiler_params=params(),
        name="prep",
    )(hist_len, block_mask, hist)


def norm_kernel(rows_ref, out_ref):
    total = rows_ref.shape[0]
    for start in range(0, total, PIECE):
        values = rows_ref[start : start + PIECE, :].astype(F32)
        centred = values - jnp.mean(values, axis=-1, keepdims=True)
        variance = jnp.mean(centred * centred, axis=-1, keepdims=True)
        out_ref[start : start + PIECE, :] = (centred * lax.rsqrt(variance + 1e-05)).astype(BF)


def norm(rows):
    vmem = pl.BlockSpec(memory_space=pltpu.VMEM)
    return pl.pallas_call(
        norm_kernel,
        in_specs=[vmem],
        out_specs=vmem,
        out_shape=jax.ShapeDtypeStruct(rows.shape, BF),
        compiler_params=params(),
        name="norm",
    )(rows)


def query_kernel(slot_ref, rows_ref, mine_ref, other_ref, out_ref):
    rows = rows_ref[...]
    share = mine_ref.shape[0] // NY
    for part, weights in enumerate((mine_ref, other_ref)):
        for pair in range(2):
            block = jnp.concatenate(
                [weights[(2 * pair + k) * share : (2 * pair + k) * share + HEAD, :] for k in range(2)]
            )
            made = lax.dot_general(rows, block, NT, preferred_element_type=F32)
            made = half_silu(made * 0.5).astype(BF)
            for lane in range(2):
                slot = slot_ref[part * 4 + pair * 2 + lane]
                out_ref[slot] = made[:, lane * HEAD : (lane + 1) * HEAD]


def query(slots, normed, mine, other):
    vmem = pl.BlockSpec(memory_space=pltpu.VMEM)
    return pl.pallas_call(
        query_kernel,
        in_specs=[pl.BlockSpec(memory_space=pltpu.SMEM), vmem, vmem, vmem],
        out_specs=vmem,
        out_shape=jax.ShapeDtypeStruct((HEADS, normed.shape[0], HEAD), BF),
        compiler_params=params(),
        name="query",
    )(slots, normed, mine, other)


def attend_kernel(scale, first, user_ref, query_ref, cache_ref, out_ref):
    sources, rows, _ = out_ref.shape

    def step(t, carry):
        users = [user_ref[s, first + t] for s in range(sources)]
        here = pl.ds(pl.multiple_of((first + t) * TILE, TILE), TILE)
        there = pl.ds(pl.multiple_of(t * TILE, TILE), TILE)
        weights = []
        for s, u in enumerate(users):
            turned = jnp.concatenate(
                [cache_ref[u, b : b + BLK, :] for b in range(0, HIST, BLK)], axis=1
            )
            score = jnp.dot(query_ref[s, here, :], turned, preferred_element_type=F32)
            weights.append(half_silu(score * (0.5 * scale)).astype(BF))
        for s, u in enumerate(users):
            out_ref[s, there, :] = jnp.dot(
                weights[s], cache_ref[u, HIST:, :], preferred_element_type=F32
            ).astype(BF)
        return carry

    lax.fori_loop(0, rows // TILE, step, 0, unroll=2)


def attend(users, queries, caches, chunk, scale):
    sources, rows, _ = queries.shape
    rows = rows // CHUNKS
    vmem = pl.BlockSpec(memory_space=pltpu.VMEM)
    smem = pl.BlockSpec(memory_space=pltpu.SMEM)
    return pl.pallas_call(
        functools.partial(attend_kernel, scale, chunk * rows // TILE),
        in_specs=[smem, vmem, vmem],
        out_specs=vmem,
        out_shape=jax.ShapeDtypeStruct((sources, rows, HEAD), BF),
        compiler_params=params(),
        name="attend",
    )(users, queries, caches)


def own_kernel(scale, rows_ref, query_ref, key_w, value_w, gate_w, own_ref, gate_ref):
    rows = rows_ref[...]
    width = rows.shape[1]

    def project(weights):
        block = weights[...].reshape(2 * HEAD, width)
        made = lax.dot_general(rows, block, NT, preferred_element_type=F32)
        return half_silu(made * 0.5).astype(BF)

    self_keys = project(key_w).astype(F32)
    self_values = project(value_w).astype(F32)
    gate_ref[...] = project(gate_w)
    for lane in range(2):
        cut = slice(lane * HEAD, (lane + 1) * HEAD)
        products = query_ref[lane].astype(F32) * self_keys[:, cut]
        strength = half_silu(jnp.sum(products, axis=1, keepdims=True) * (0.5 * scale))
        own_ref[:, cut] = strength * self_values[:, cut]


def own(normed, queries, gathered, scale):
    total, width = normed.shape
    steps = width // (2 * HEAD)

    def weights(place):
        return pl.BlockSpec((2, HEAD, width), lambda i: (place * steps + i, 0, 0))

    return pl.pallas_call(
        functools.partial(own_kernel, scale),
        grid=(steps,),
        in_specs=[
            pl.BlockSpec((total, width), lambda i: (0, 0)),
            pl.BlockSpec((2, total, HEAD), lambda i: (i, 0, 0)),
            weights(1),
            weights(2),
            weights(3),
        ],
        out_specs=[pl.BlockSpec((total, 2 * HEAD), lambda i: (0, i))] * 2,
        out_shape=[
            jax.ShapeDtypeStruct((total, width), F32),
            jax.ShapeDtypeStruct((total, width), BF),
        ],
        compiler_params=params(56),
        name="own",
    )(normed, queries, gathered, gathered, gathered)


def finish_kernel(first, count_ref, hist_ref, own_ref, gate_ref, out_w, rows_ref, *rest):
    out_ref = rest[-1]
    rows, width = rows_ref.shape
    history = jnp.concatenate([hist_ref[h].astype(F32) for h in range(HEADS)], axis=1)
    combined = history + own_ref[...]
    centred = combined - jnp.mean(combined, axis=-1, keepdims=True)
    variance = jnp.mean(centred * centred, axis=-1, keepdims=True)
    gated = centred * lax.rsqrt(variance + 1e-05) * gate_ref[...].astype(F32)
    mixed = jnp.dot(gated.astype(BF), out_w[...], preferred_element_type=F32)
    mixed = mixed + rows_ref[...].astype(F32)
    slot = lax.broadcasted_iota(jnp.int32, (TILE, width), 0)
    tile = (first + pl.program_id(0)) * (rows // TILE)
    for t in range(rows // TILE):
        cut = slice(t * TILE, (t + 1) * TILE)
        scored = jnp.where(slot < count_ref[tile + t], mixed[cut, :], 0.0)
        out_ref[cut, :] = scored.astype(BF)


def finish(counts, history, own_part, gate, out_w, candidates, chunk, before):
    total, width = candidates.shape
    steps = total // CHUNKS // PIECE
    place = pl.BlockSpec((PIECE, width), lambda i: (chunk * steps + i, 0))
    specs = [
        pl.BlockSpec(memory_space=pltpu.SMEM),
        pl.BlockSpec((HEADS, PIECE, HEAD), lambda i: (0, i, 0)),
        place,
        place,
        pl.BlockSpec((width, width), lambda i: (0, 0)),
        place,
    ]
    given = [counts, history, own_part, gate, out_w, candidates]
    aliases = {}
    if before is not None:
        specs.append(pl.BlockSpec(memory_space=pl.ANY))
        given.append(before)
        aliases = {len(given) - 1: 0}
    return pl.pallas_call(
        functools.partial(finish_kernel, chunk * steps),
        grid=(steps,),
        in_specs=specs,
        out_specs=place,
        out_shape=jax.ShapeDtypeStruct((total, width), BF),
        input_output_aliases=aliases,
        compiler_params=params(56),
        name="finish",
    )(*given)


def swap_z(values):
    return lax.all_to_all(values, "z", split_axis=0, concat_axis=0, tiled=True)


def spread_y(part):
    up = lax.ppermute(part, "y", ring(NY, 1))
    down = lax.ppermute(part, "y", ring(NY, NY - 1))
    half = part.shape[0] // 2
    far = [
        lax.ppermute(up[:half], "y", ring(NY, 1)),
        lax.ppermute(down[half:], "y", ring(NY, NY - 1)),
    ]
    return jnp.concatenate([part, up] + far + [down], axis=0)


def shards(candidates, hist_kv, hist_len, block_mask, tile_user, tile_count, weight_in, weight_out):
    width = candidates.shape[1]
    tiles = tile_user.shape[0]
    scale = HEAD ** (-0.5)
    at_x, at_core, at_y, at_z = [lax.axis_index(name) for name in ("x", "core", "y", "z")]

    columns = weight_in.T
    share, out_share = columns.shape[0], weight_out.shape[0]
    normed = norm(candidates)
    caches = swap_z(prep(hist_kv[0], hist_len, block_mask))
    both = jnp.concatenate([columns, weight_out], axis=0)
    sent = [lax.ppermute(both, "x", [(0, k), (k, 0)]) for k in range(1, NX)]
    query_part = jnp.where(at_x == 0, columns, sent[0][:share] + sent[1][:share] + sent[2][:share])
    out_part = jnp.concatenate([weight_out] + [piece[share:] for piece in sent], axis=0)
    rest_part = jnp.where(at_x == 0, out_part, columns)
    meta = jnp.zeros((META, width), BF).at[0, :tiles].set(tile_user[:, 0].astype(BF))
    packed = jnp.concatenate([query_part, rest_part, meta], axis=0)
    spread = [packed] + [lax.ppermute(packed, "z", ring(NZ, k)) for k in range(1, NZ)]
    spread, caches, normed = lax.optimization_barrier((spread, caches, normed))
    caches = lax.all_gather(caches, "y", axis=0, tiled=True)
    spread = jnp.stack(spread)[(at_z - jnp.arange(NZ, dtype=jnp.int32)) % NZ]
    query_z = spread[:, :share].reshape(NZ * share, width)
    users = spread[:, 2 * share, :tiles].astype(jnp.int32)
    rest = spread[:, share : 2 * share].reshape(NZ * share, width)

    parts = [query_z] + [lax.ppermute(query_z, "y", ring(NY, k)) for k in range(1, NY)]
    mine = jnp.concatenate(parts, axis=0)
    other = lax.ppermute(mine, "core", ring(NC, 1))
    at = (at_y - jnp.arange(NY, dtype=jnp.int32)) % NY
    slots = jnp.concatenate([at_core * NY + at, (1 - at_core) * NY + at]).astype(jnp.int32)

    queries = query(slots, normed, mine, other)
    arrived = swap_z(queries)
    rest = [rest] + [lax.ppermute(rest, "y", ring(NY, k)) for k in range(1, NY)]
    rest = jnp.stack(rest)[at]
    rest, arrived = lax.optimization_barrier((rest, arrived))
    gathered = lax.all_gather(rest, ("x", "core"), axis=0, tiled=True)

    history = [swap_z(attend(users, arrived, caches, c, scale)) for c in range(CHUNKS)]
    out_w = gathered[:HEADS].reshape(NC * NY * NZ, NX, -1, width)
    out_w = jnp.swapaxes(out_w, 0, 1).reshape(width, width)
    own_part, gate = own(normed, queries, gathered, scale)
    out = None
    for c in range(CHUNKS):
        out = finish(tile_count, history[c], own_part, gate, out_w, candidates, c, out)
    return out


def solution(mesh):
    fine = Mesh(mesh.devices.reshape(NX, NC, NY, NZ), ("x", "core", "y", "z"))
    every = ("x", "core", "y", "z")
    in_specs = (
        P(every, None),
        P(every, None, None),
        P(every),
        P(every, None),
        P(every, None),
        P(every),
        P(None, every),
        P(every, None),
    )
    return jax.shard_map(
        shards, mesh=fine, in_specs=in_specs, out_specs=P(every, None), check_vma=False
    )
```

```python
import functools

import jax
import jax.numpy as jnp
from jax import lax
from jax.experimental import pallas as pl
from jax.experimental.pallas import tpu as pltpu
from jax.sharding import Mesh
from jax.sharding import PartitionSpec as P

HEADS = 8
HEAD = 128
BLK = 128
HIST = 384
TILE = 64
META = 8
PIECE = 512
NX, NC, NY, NZ = 4, 2, 4, 8
BF = jnp.bfloat16
F32 = jnp.float32
MIB = 1024 * 1024
NT = (((1,), (1,)), ((), ()))


def half_silu(a):
    return a + a * jnp.tanh(a)


def params(limit=16):
    return pltpu.CompilerParams(vmem_limit_bytes=limit * MIB)


def ring(size, step):
    return [(i, (i + step) % size) for i in range(size)]


def prep_kernel(len_ref, mask_ref, hist_ref, out_ref):
    place = lax.broadcasted_iota(jnp.int32, (HIST, HEAD), 0)
    kept = jnp.where(
        place < BLK, mask_ref[0, 0], jnp.where(place < 2 * BLK, mask_ref[0, 1], mask_ref[0, 2])
    )
    live = (place < len_ref[0]) & (kept > 0)
    width = HEADS * HEAD
    for h in range(HEADS):
        cut = slice(h * HEAD, (h + 1) * HEAD)
        for b in range(0, HIST, BLK):
            turned = hist_ref[b : b + BLK, cut].astype(F32).T
            out_ref[h, b : b + BLK, :] = turned.astype(BF)
        values = hist_ref[:, width + h * HEAD : width + (h + 1) * HEAD].astype(F32)
        out_ref[h, HIST:, :] = jnp.where(live, values, 0.0).astype(BF)


def prep(hist, hist_len, block_mask):
    smem = pl.BlockSpec(memory_space=pltpu.SMEM)
    vmem = pl.BlockSpec(memory_space=pltpu.VMEM)
    return pl.pallas_call(
        prep_kernel,
        in_specs=[smem, smem, vmem],
        out_specs=vmem,
        out_shape=jax.ShapeDtypeStruct((HEADS, 2 * HIST, HEAD), BF),
        compiler_params=params(),
        name="prep",
    )(hist_len, block_mask, hist)


def norm_kernel(rows_ref, out_ref):
    total = rows_ref.shape[0]
    for start in range(0, total, PIECE):
        values = rows_ref[start : start + PIECE, :].astype(F32)
        centred = values - jnp.mean(values, axis=-1, keepdims=True)
        variance = jnp.mean(centred * centred, axis=-1, keepdims=True)
        out_ref[start : start + PIECE, :] = (centred * lax.rsqrt(variance + 1e-05)).astype(BF)


def norm(rows):
    vmem = pl.BlockSpec(memory_space=pltpu.VMEM)
    return pl.pallas_call(
        norm_kernel,
        in_specs=[vmem],
        out_specs=vmem,
        out_shape=jax.ShapeDtypeStruct(rows.shape, BF),
        compiler_params=params(),
        name="norm",
    )(rows)


def query_kernel(slot_ref, rows_ref, mine_ref, other_ref, out_ref):
    rows = rows_ref[...]
    share = mine_ref.shape[0] // NY
    for part, weights in enumerate((mine_ref, other_ref)):
        for pair in range(2):
            block = jnp.concatenate(
                [weights[(2 * pair + k) * share : (2 * pair + k) * share + HEAD, :] for k in range(2)]
            )
            made = lax.dot_general(rows, block, NT, preferred_element_type=F32)
            made = half_silu(made * 0.5).astype(BF)
            for lane in range(2):
                slot = slot_ref[part * 4 + pair * 2 + lane]
                out_ref[slot] = made[:, lane * HEAD : (lane + 1) * HEAD]


def query(slots, normed, mine, other):
    vmem = pl.BlockSpec(memory_space=pltpu.VMEM)
    return pl.pallas_call(
        query_kernel,
        in_specs=[pl.BlockSpec(memory_space=pltpu.SMEM), vmem, vmem, vmem],
        out_specs=vmem,
        out_shape=jax.ShapeDtypeStruct((HEADS, normed.shape[0], HEAD), BF),
        compiler_params=params(),
        name="query",
    )(slots, normed, mine, other)


def attend_kernel(scale, user_ref, query_ref, cache_ref, out_ref):
    sources, rows, _ = out_ref.shape

    def step(t, carry):
        users = [user_ref[s, t] for s in range(sources)]
        here = pl.ds(pl.multiple_of(t * TILE, TILE), TILE)
        weights = []
        for s, u in enumerate(users):
            turned = jnp.concatenate(
                [cache_ref[u, b : b + BLK, :] for b in range(0, HIST, BLK)], axis=1
            )
            score = jnp.dot(query_ref[s, here, :], turned, preferred_element_type=F32)
            weights.append(half_silu(score * (0.5 * scale)).astype(BF))
        for s, u in enumerate(users):
            out_ref[s, here, :] = jnp.dot(
                weights[s], cache_ref[u, HIST:, :], preferred_element_type=F32
            ).astype(BF)
        return carry

    lax.fori_loop(0, rows // TILE, step, 0, unroll=2)


def attend(users, queries, caches, scale):
    vmem = pl.BlockSpec(memory_space=pltpu.VMEM)
    smem = pl.BlockSpec(memory_space=pltpu.SMEM)
    return pl.pallas_call(
        functools.partial(attend_kernel, scale),
        in_specs=[smem, vmem, vmem],
        out_specs=vmem,
        out_shape=jax.ShapeDtypeStruct(queries.shape, BF),
        compiler_params=params(),
        name="attend",
    )(users, queries, caches)


def own_kernel(scale, rows_ref, query_ref, key_w, value_w, gate_w, own_ref, gate_ref):
    rows = rows_ref[...]
    width = rows.shape[1]

    def project(weights):
        block = weights[...].reshape(2 * HEAD, width)
        made = lax.dot_general(rows, block, NT, preferred_element_type=F32)
        return half_silu(made * 0.5).astype(BF)

    self_keys = project(key_w).astype(F32)
    self_values = project(value_w).astype(F32)
    gate_ref[...] = project(gate_w)
    for lane in range(2):
        cut = slice(lane * HEAD, (lane + 1) * HEAD)
        products = query_ref[lane].astype(F32) * self_keys[:, cut]
        strength = half_silu(jnp.sum(products, axis=1, keepdims=True) * (0.5 * scale))
        own_ref[:, cut] = strength * self_values[:, cut]


def own(normed, queries, gathered, scale):
    total, width = normed.shape
    steps = width // (2 * HEAD)

    def weights(place):
        return pl.BlockSpec((2, HEAD, width), lambda i: (place * steps + i, 0, 0))

    return pl.pallas_call(
        functools.partial(own_kernel, scale),
        grid=(steps,),
        in_specs=[
            pl.BlockSpec((total, width), lambda i: (0, 0)),
            pl.BlockSpec((2, total, HEAD), lambda i: (i, 0, 0)),
            weights(1),
            weights(2),
            weights(3),
        ],
        out_specs=[pl.BlockSpec((total, 2 * HEAD), lambda i: (0, i))] * 2,
        out_shape=[
            jax.ShapeDtypeStruct((total, width), F32),
            jax.ShapeDtypeStruct((total, width), BF),
        ],
        compiler_params=params(56),
        name="own",
    )(normed, queries, gathered, gathered, gathered)


def turn_kernel(gathered, out_ref):
    shares, rows, _ = gathered.shape
    piece = rows // (NX * NZ)
    to = lax.broadcasted_iota(jnp.int32, (rows, rows), 0)
    at = lax.broadcasted_iota(jnp.int32, (rows, rows), 1)
    plane, place, line = to // (NZ * piece), to // piece % NZ, to % piece
    picked = (at == (place * NX + plane) * piece + line).astype(F32).astype(BF)
    span = rows // NX
    for i in range(shares):
        turned = jnp.dot(picked, gathered[i], preferred_element_type=F32).astype(BF)
        for k in range(NX):
            first = (k * shares + i) * span
            out_ref[first : first + span, :] = turned[k * span : (k + 1) * span, :]


def turn(gathered):
    rows, width = gathered.shape[1:]
    return pl.pallas_call(
        turn_kernel,
        grid=(1,),
        in_specs=[pl.BlockSpec((HEADS, rows, width), lambda i: (0, 0, 0))],
        out_specs=pl.BlockSpec((width, width), lambda i: (0, 0)),
        out_shape=jax.ShapeDtypeStruct((width, width), BF),
        compiler_params=params(56),
        name="turn",
    )(gathered)


def finish_kernel(count_ref, hist_ref, own_ref, gate_ref, out_w, rows_ref, out_ref):
    rows, width = rows_ref.shape
    history = jnp.concatenate([hist_ref[h].astype(F32) for h in range(HEADS)], axis=1)
    combined = history + own_ref[...]
    centred = combined - jnp.mean(combined, axis=-1, keepdims=True)
    variance = jnp.mean(centred * centred, axis=-1, keepdims=True)
    gated = centred * lax.rsqrt(variance + 1e-05) * gate_ref[...].astype(F32)
    mixed = jnp.dot(gated.astype(BF), out_w[...], preferred_element_type=F32)
    mixed = mixed + rows_ref[...].astype(F32)
    slot = lax.broadcasted_iota(jnp.int32, (TILE, width), 0)
    tile = pl.program_id(0) * (rows // TILE)
    for t in range(rows // TILE):
        cut = slice(t * TILE, (t + 1) * TILE)
        scored = jnp.where(slot < count_ref[tile + t], mixed[cut, :], 0.0)
        out_ref[cut, :] = scored.astype(BF)


def finish(counts, history, own_part, gate, out_w, candidates):
    total, width = candidates.shape
    place = pl.BlockSpec((PIECE, width), lambda i: (i, 0))
    return pl.pallas_call(
        finish_kernel,
        grid=(total // PIECE,),
        in_specs=[
            pl.BlockSpec(memory_space=pltpu.SMEM),
            pl.BlockSpec((HEADS, PIECE, HEAD), lambda i: (0, i, 0)),
            place,
            place,
            pl.BlockSpec((width, width), lambda i: (0, 0)),
            place,
        ],
        out_specs=place,
        out_shape=jax.ShapeDtypeStruct((total, width), BF),
        compiler_params=params(56),
        name="finish",
    )(counts, history, own_part, gate, out_w, candidates)


def swap_z(values):
    return lax.all_to_all(values, "z", split_axis=0, concat_axis=0, tiled=True)


def spread_y(part):
    up = lax.ppermute(part, "y", ring(NY, 1))
    down = lax.ppermute(part, "y", ring(NY, NY - 1))
    half = part.shape[0] // 2
    far = [
        lax.ppermute(up[:half], "y", ring(NY, 1)),
        lax.ppermute(down[half:], "y", ring(NY, NY - 1)),
    ]
    return jnp.concatenate([part, up] + far + [down], axis=0)


def shards(candidates, hist_kv, hist_len, block_mask, tile_user, tile_count, weight_in, weight_out):
    width = candidates.shape[1]
    tiles = tile_user.shape[0]
    scale = HEAD ** (-0.5)
    at_x, at_core, at_y, at_z = [lax.axis_index(name) for name in ("x", "core", "y", "z")]

    columns = weight_in.T
    share, out_share = columns.shape[0], weight_out.shape[0]
    normed = norm(candidates)
    caches = swap_z(prep(hist_kv[0], hist_len, block_mask))
    both = jnp.concatenate([columns, weight_out], axis=0)
    sent = [lax.ppermute(both, "x", [(0, k), (k, 0)]) for k in range(1, NX)]
    query_part = jnp.where(at_x == 0, columns, sent[0][:share] + sent[1][:share] + sent[2][:share])
    out_part = jnp.concatenate([weight_out] + [piece[share:] for piece in sent], axis=0)
    rest_part = jnp.where(at_x == 0, out_part, columns)
    meta = jnp.zeros((META, width), BF).at[0, :tiles].set(tile_user[:, 0].astype(BF))
    packed = jnp.concatenate([query_part, rest_part, meta], axis=0)
    spread = [packed] + [lax.ppermute(packed, "z", ring(NZ, k)) for k in range(1, NZ)]
    spread, caches, normed = lax.optimization_barrier((spread, caches, normed))
    caches = lax.all_gather(caches, "y", axis=0, tiled=True)
    spread = jnp.stack(spread)[(at_z - jnp.arange(NZ, dtype=jnp.int32)) % NZ]
    query_z = spread[:, :share].reshape(NZ * share, width)
    users = spread[:, 2 * share, :tiles].astype(jnp.int32)
    rest = spread[:, share : 2 * share].reshape(NZ * share, width)

    parts = [query_z] + [lax.ppermute(query_z, "y", ring(NY, k)) for k in range(1, NY)]
    mine = jnp.concatenate(parts, axis=0)
    other = lax.ppermute(mine, "core", ring(NC, 1))
    at = (at_y - jnp.arange(NY, dtype=jnp.int32)) % NY
    slots = jnp.concatenate([at_core * NY + at, (1 - at_core) * NY + at]).astype(jnp.int32)

    queries = query(slots, normed, mine, other)
    rest, queries = lax.optimization_barrier((rest, queries))
    arrived = swap_z(queries)
    gathered = lax.all_gather(rest, ("x", "core", "y"))

    history = swap_z(attend(users, arrived, caches, scale))
    out_w = turn(gathered)
    own_part, gate = own(normed, queries, gathered, scale)
    return finish(tile_count, history, own_part, gate, out_w, candidates)


def solution(mesh):
    fine = Mesh(mesh.devices.reshape(NX, NC, NY, NZ), ("x", "core", "y", "z"))
    every = ("x", "core", "y", "z")
    in_specs = (
        P(every, None),
        P(every, None, None),
        P(every),
        P(every, None),
        P(every, None),
        P(every),
        P(None, every),
        P(every, None),
    )
    return jax.shard_map(
        shards, mesh=fine, in_specs=in_specs, out_specs=P(every, None), check_vma=False
    )
```

```python
import functools

import jax
import jax.numpy as jnp
from jax import lax
from jax.experimental import pallas as pl
from jax.experimental.pallas import tpu as pltpu
from jax.sharding import Mesh
from jax.sharding import PartitionSpec as P

HEADS = 8
HEAD = 128
BLK = 128
HIST = 384
TILE = 64
META = 16
PIECE = 512
NX, NC, NY, NZ = 4, 2, 4, 8
BF = jnp.bfloat16
F32 = jnp.float32
MIB = 1024 * 1024
NT = (((1,), (1,)), ((), ()))


def half_silu(a):
    return a + a * jnp.tanh(a)


def params(limit=16):
    return pltpu.CompilerParams(vmem_limit_bytes=limit * MIB)


def ring(size, step):
    return [(i, (i + step) % size) for i in range(size)]


def prep_kernel(len_ref, mask_ref, hist_ref, meta_ref, out_ref):
    place = lax.broadcasted_iota(jnp.int32, (HIST, HEAD), 0)
    kept = jnp.where(
        place < BLK, mask_ref[0, 0], jnp.where(place < 2 * BLK, mask_ref[0, 1], mask_ref[0, 2])
    )
    live = (place < len_ref[0]) & (kept > 0)
    width = HEADS * HEAD
    for h in range(HEADS):
        cut = slice(h * HEAD, (h + 1) * HEAD)
        for b in range(0, HIST, BLK):
            turned = hist_ref[b : b + BLK, cut].astype(F32).T
            out_ref[h, b : b + BLK, :] = turned.astype(BF)
        values = hist_ref[:, width + h * HEAD : width + (h + 1) * HEAD].astype(F32)
        out_ref[h, HIST : 2 * HIST, :] = jnp.where(live, values, 0.0).astype(BF)
        out_ref[h, 2 * HIST :, :] = meta_ref[...]


def prep(hist, hist_len, block_mask, meta):
    smem = pl.BlockSpec(memory_space=pltpu.SMEM)
    vmem = pl.BlockSpec(memory_space=pltpu.VMEM)
    return pl.pallas_call(
        prep_kernel,
        in_specs=[smem, smem, vmem, vmem],
        out_specs=vmem,
        out_shape=jax.ShapeDtypeStruct((HEADS, 2 * HIST + META, HEAD), BF),
        compiler_params=params(),
        name="prep",
    )(hist_len, block_mask, hist, meta)


def norm_kernel(rows_ref, out_ref):
    total = rows_ref.shape[0]
    for start in range(0, total, PIECE):
        values = rows_ref[start : start + PIECE, :].astype(F32)
        centred = values - jnp.mean(values, axis=-1, keepdims=True)
        variance = jnp.mean(centred * centred, axis=-1, keepdims=True)
        out_ref[start : start + PIECE, :] = (centred * lax.rsqrt(variance + 1e-05)).astype(BF)


def norm(rows):
    vmem = pl.BlockSpec(memory_space=pltpu.VMEM)
    return pl.pallas_call(
        norm_kernel,
        in_specs=[vmem],
        out_specs=vmem,
        out_shape=jax.ShapeDtypeStruct(rows.shape, BF),
        compiler_params=params(),
        name="norm",
    )(rows)


def query_kernel(slot_ref, rows_ref, mine_ref, other_ref, out_ref):
    rows = rows_ref[...]
    share = mine_ref.shape[0] // NY
    for part, weights in enumerate((mine_ref, other_ref)):
        for pair in range(2):
            block = jnp.concatenate(
                [weights[(2 * pair + k) * share : (2 * pair + k) * share + HEAD, :] for k in range(2)]
            )
            made = lax.dot_general(rows, block, NT, preferred_element_type=F32)
            made = half_silu(made * 0.5).astype(BF)
            for lane in range(2):
                slot = slot_ref[part * 4 + pair * 2 + lane]
                out_ref[slot] = made[:, lane * HEAD : (lane + 1) * HEAD]


def query(slots, normed, mine, other):
    vmem = pl.BlockSpec(memory_space=pltpu.VMEM)
    return pl.pallas_call(
        query_kernel,
        in_specs=[pl.BlockSpec(memory_space=pltpu.SMEM), vmem, vmem, vmem],
        out_specs=vmem,
        out_shape=jax.ShapeDtypeStruct((HEADS, normed.shape[0], HEAD), BF),
        compiler_params=params(),
        name="query",
    )(slots, normed, mine, other)


def attend_kernel(scale, user_ref, query_ref, cache_ref, out_ref):
    sources, rows, _ = out_ref.shape

    def step(t, carry):
        users = [user_ref[s, t] for s in range(sources)]
        here = pl.ds(pl.multiple_of(t * TILE, TILE), TILE)
        weights = []
        for s, u in enumerate(users):
            turned = jnp.concatenate(
                [cache_ref[u, b : b + BLK, :] for b in range(0, HIST, BLK)], axis=1
            )
            score = jnp.dot(query_ref[s, here, :], turned, preferred_element_type=F32)
            weights.append(half_silu(score * (0.5 * scale)).astype(BF))
        for s, u in enumerate(users):
            out_ref[s, here, :] = jnp.dot(
                weights[s], cache_ref[u, HIST : 2 * HIST, :], preferred_element_type=F32
            ).astype(BF)
        return carry

    lax.fori_loop(0, rows // TILE, step, 0, unroll=4)


def attend(users, queries, caches, scale):
    vmem = pl.BlockSpec(memory_space=pltpu.VMEM)
    smem = pl.BlockSpec(memory_space=pltpu.SMEM)
    return pl.pallas_call(
        functools.partial(attend_kernel, scale),
        in_specs=[smem, vmem, vmem],
        out_specs=vmem,
        out_shape=jax.ShapeDtypeStruct(queries.shape, BF),
        compiler_params=params(),
        name="attend",
    )(users, queries, caches)


def own_kernel(scale, rows_ref, query_ref, key_w, value_w, gate_w, own_ref, gate_ref):
    rows = rows_ref[...]
    width = rows.shape[1]

    def project(weights):
        block = weights[...].reshape(2 * HEAD, width)
        made = lax.dot_general(rows, block, NT, preferred_element_type=F32)
        return half_silu(made * 0.5).astype(BF)

    self_keys = project(key_w).astype(F32)
    self_values = project(value_w).astype(F32)
    gate_ref[...] = project(gate_w)
    for lane in range(2):
        cut = slice(lane * HEAD, (lane + 1) * HEAD)
        products = query_ref[lane].astype(F32) * self_keys[:, cut]
        strength = half_silu(jnp.sum(products, axis=1, keepdims=True) * (0.5 * scale))
        own_ref[:, cut] = strength * self_values[:, cut]


def own(normed, queries, gathered, scale):
    total, width = normed.shape
    steps = width // (2 * HEAD)

    def weights(place):
        return pl.BlockSpec((2, HEAD, width), lambda i: (place * steps + i, 0, 0))

    return pl.pallas_call(
        functools.partial(own_kernel, scale),
        grid=(steps,),
        in_specs=[
            pl.BlockSpec((total, width), lambda i: (0, 0)),
            pl.BlockSpec((2, total, HEAD), lambda i: (i, 0, 0)),
            weights(1),
            weights(2),
            weights(3),
        ],
        out_specs=[pl.BlockSpec((total, 2 * HEAD), lambda i: (0, i))] * 2,
        out_shape=[
            jax.ShapeDtypeStruct((total, width), F32),
            jax.ShapeDtypeStruct((total, width), BF),
        ],
        compiler_params=params(56),
        name="own",
    )(normed, queries, gathered, gathered, gathered)


def turn_kernel(gathered, out_ref):
    shares, rows, _ = gathered.shape
    piece = rows // (NX * NZ)
    to = lax.broadcasted_iota(jnp.int32, (rows, rows), 0)
    at = lax.broadcasted_iota(jnp.int32, (rows, rows), 1)
    plane, place, line = to // (NZ * piece), to // piece % NZ, to % piece
    picked = (at == (place * NX + plane) * piece + line).astype(F32).astype(BF)
    span = rows // NX
    for i in range(shares):
        turned = jnp.dot(picked, gathered[i], preferred_element_type=F32).astype(BF)
        for k in range(NX):
            first = (k * shares + i) * span
            out_ref[first : first + span, :] = turned[k * span : (k + 1) * span, :]


def turn(gathered):
    rows, width = gathered.shape[1:]
    return pl.pallas_call(
        turn_kernel,
        grid=(1,),
        in_specs=[pl.BlockSpec((HEADS, rows, width), lambda i: (0, 0, 0))],
        out_specs=pl.BlockSpec((width, width), lambda i: (0, 0)),
        out_shape=jax.ShapeDtypeStruct((width, width), BF),
        compiler_params=params(56),
        name="turn",
    )(gathered)


def finish_kernel(count_ref, hist_ref, own_ref, gate_ref, out_w, rows_ref, out_ref):
    rows, width = rows_ref.shape
    history = jnp.concatenate([hist_ref[h].astype(F32) for h in range(HEADS)], axis=1)
    combined = history + own_ref[...]
    centred = combined - jnp.mean(combined, axis=-1, keepdims=True)
    variance = jnp.mean(centred * centred, axis=-1, keepdims=True)
    gated = centred * lax.rsqrt(variance + 1e-05) * gate_ref[...].astype(F32)
    mixed = jnp.dot(gated.astype(BF), out_w[...], preferred_element_type=F32)
    mixed = mixed + rows_ref[...].astype(F32)
    slot = lax.broadcasted_iota(jnp.int32, (TILE, width), 0)
    tile = pl.program_id(0) * (rows // TILE)
    for t in range(rows // TILE):
        cut = slice(t * TILE, (t + 1) * TILE)
        scored = jnp.where(slot < count_ref[tile + t], mixed[cut, :], 0.0)
        out_ref[cut, :] = scored.astype(BF)


def finish(counts, history, own_part, gate, out_w, candidates):
    total, width = candidates.shape
    place = pl.BlockSpec((PIECE, width), lambda i: (i, 0))
    return pl.pallas_call(
        finish_kernel,
        grid=(total // PIECE,),
        in_specs=[
            pl.BlockSpec(memory_space=pltpu.SMEM),
            pl.BlockSpec((HEADS, PIECE, HEAD), lambda i: (0, i, 0)),
            place,
            place,
            pl.BlockSpec((width, width), lambda i: (0, 0)),
            place,
        ],
        out_specs=place,
        out_shape=jax.ShapeDtypeStruct((total, width), BF),
        compiler_params=params(56),
        name="finish",
    )(counts, history, own_part, gate, out_w, candidates)


def swap_z(values):
    return lax.all_to_all(values, "z", split_axis=0, concat_axis=0, tiled=True)


def spread_y(part):
    up = lax.ppermute(part, "y", ring(NY, 1))
    down = lax.ppermute(part, "y", ring(NY, NY - 1))
    half = part.shape[0] // 2
    far = [
        lax.ppermute(up[:half], "y", ring(NY, 1)),
        lax.ppermute(down[half:], "y", ring(NY, NY - 1)),
    ]
    return jnp.concatenate([part, up] + far + [down], axis=0)


def shards(candidates, hist_kv, hist_len, block_mask, tile_user, tile_count, weight_in, weight_out):
    width = candidates.shape[1]
    tiles = tile_user.shape[0]
    scale = HEAD ** (-0.5)
    at_x, at_core, at_y, at_z = [lax.axis_index(name) for name in ("x", "core", "y", "z")]

    columns = weight_in.T
    share, out_share = columns.shape[0], weight_out.shape[0]
    normed = norm(candidates)
    meta = jnp.zeros((META, HEAD), BF).at[0, :tiles].set(tile_user[:, 0].astype(BF))
    caches = swap_z(prep(hist_kv[0], hist_len, block_mask, meta))
    both = jnp.concatenate([columns, weight_out], axis=0)
    sent = [lax.ppermute(both, "x", [(0, k), (k, 0)]) for k in range(1, NX)]
    query_part = jnp.where(at_x == 0, columns, sent[0][:share] + sent[1][:share] + sent[2][:share])
    out_part = jnp.concatenate([weight_out] + [piece[share:] for piece in sent], axis=0)
    rest_part = jnp.where(at_x == 0, out_part, columns)
    packed = jnp.concatenate([query_part, rest_part], axis=0)
    spread = [packed] + [lax.ppermute(packed, "z", ring(NZ, k)) for k in range(1, NZ)]
    spread, caches, normed = lax.optimization_barrier((spread, caches, normed))
    users = caches[:, 2 * HIST, :tiles].astype(jnp.int32)
    caches = lax.all_gather(caches, "y", axis=0, tiled=True)
    spread = jnp.stack(spread)[(at_z - jnp.arange(NZ, dtype=jnp.int32)) % NZ]
    query_z = spread[:, :share].reshape(NZ * share, width)
    rest = spread[:, share : 2 * share].reshape(NZ * share, width)

    parts = [query_z] + [lax.ppermute(query_z, "y", ring(NY, k)) for k in range(1, NY)]
    mine = jnp.concatenate(parts, axis=0)
    other = lax.ppermute(mine, "core", ring(NC, 1))
    at = (at_y - jnp.arange(NY, dtype=jnp.int32)) % NY
    slots = jnp.concatenate([at_core * NY + at, (1 - at_core) * NY + at]).astype(jnp.int32)

    queries = query(slots, normed, mine, other)
    rest, queries = lax.optimization_barrier((rest, queries))
    arrived = swap_z(queries)
    gathered = lax.all_gather(rest, ("x", "core", "y"))

    history = swap_z(attend(users, arrived, caches, scale))
    out_w = turn(gathered)
    own_part, gate = own(normed, queries, gathered, scale)
    return finish(tile_count, history, own_part, gate, out_w, candidates)


def solution(mesh):
    fine = Mesh(mesh.devices.reshape(NX, NC, NY, NZ), ("x", "core", "y", "z"))
    every = ("x", "core", "y", "z")
    in_specs = (
        P(every, None),
        P(every, None, None),
        P(every),
        P(every, None),
        P(every, None),
        P(every),
        P(None, every),
        P(every, None),
    )
    return jax.shard_map(
        shards, mesh=fine, in_specs=in_specs, out_specs=P(every, None), check_vma=False
    )
```

```python
import functools

import jax
import jax.numpy as jnp
from jax import lax
from jax.experimental import pallas as pl
from jax.experimental.pallas import tpu as pltpu
from jax.sharding import Mesh
from jax.sharding import PartitionSpec as P

HEADS = 8
HEAD = 128
BLK = 128
HIST = 384
TILE = 64
META = 16
PIECE = 512
NX, NC, NY, NZ = 4, 2, 4, 8
BF = jnp.bfloat16
F32 = jnp.float32
MIB = 1024 * 1024
NT = (((1,), (1,)), ((), ()))


def half_silu(a):
    return a + a * jnp.tanh(a)


def params(limit=16):
    return pltpu.CompilerParams(vmem_limit_bytes=limit * MIB)


def ring(size, step):
    return [(i, (i + step) % size) for i in range(size)]


def prep_kernel(len_ref, mask_ref, hist_ref, meta_ref, out_ref):
    place = lax.broadcasted_iota(jnp.int32, (HIST, HEAD), 0)
    kept = jnp.where(
        place < BLK, mask_ref[0, 0], jnp.where(place < 2 * BLK, mask_ref[0, 1], mask_ref[0, 2])
    )
    live = (place < len_ref[0]) & (kept > 0)
    width = HEADS * HEAD
    for h in range(HEADS):
        cut = slice(h * HEAD, (h + 1) * HEAD)
        for b in range(0, HIST, BLK):
            turned = hist_ref[b : b + BLK, cut].astype(F32).T
            out_ref[h, b : b + BLK, :] = turned.astype(BF)
        values = hist_ref[:, width + h * HEAD : width + (h + 1) * HEAD].astype(F32)
        out_ref[h, HIST : 2 * HIST, :] = jnp.where(live, values, 0.0).astype(BF)
        out_ref[h, 2 * HIST :, :] = meta_ref[...]


def prep(hist, hist_len, block_mask, meta):
    smem = pl.BlockSpec(memory_space=pltpu.SMEM)
    vmem = pl.BlockSpec(memory_space=pltpu.VMEM)
    return pl.pallas_call(
        prep_kernel,
        in_specs=[smem, smem, vmem, vmem],
        out_specs=vmem,
        out_shape=jax.ShapeDtypeStruct((HEADS, 2 * HIST + META, HEAD), BF),
        compiler_params=params(),
        name="prep",
    )(hist_len, block_mask, hist, meta)


def norm_kernel(rows_ref, out_ref):
    total = rows_ref.shape[0]
    for start in range(0, total, PIECE):
        values = rows_ref[start : start + PIECE, :].astype(F32)
        centred = values - jnp.mean(values, axis=-1, keepdims=True)
        variance = jnp.mean(centred * centred, axis=-1, keepdims=True)
        out_ref[start : start + PIECE, :] = (centred * lax.rsqrt(variance + 1e-05)).astype(BF)


def norm(rows):
    vmem = pl.BlockSpec(memory_space=pltpu.VMEM)
    return pl.pallas_call(
        norm_kernel,
        in_specs=[vmem],
        out_specs=vmem,
        out_shape=jax.ShapeDtypeStruct(rows.shape, BF),
        compiler_params=params(),
        name="norm",
    )(rows)


def query_kernel(slot_ref, rows_ref, mine_ref, other_ref, out_ref):
    rows = rows_ref[...]
    share = mine_ref.shape[0] // NY
    for part, weights in enumerate((mine_ref, other_ref)):
        for pair in range(2):
            block = jnp.concatenate(
                [weights[(2 * pair + k) * share : (2 * pair + k) * share + HEAD, :] for k in range(2)]
            )
            made = lax.dot_general(rows, block, NT, preferred_element_type=F32)
            made = half_silu(made * 0.5).astype(BF)
            for lane in range(2):
                slot = slot_ref[part * 4 + pair * 2 + lane]
                out_ref[slot] = made[:, lane * HEAD : (lane + 1) * HEAD]


def query(slots, normed, mine, other):
    vmem = pl.BlockSpec(memory_space=pltpu.VMEM)
    return pl.pallas_call(
        query_kernel,
        in_specs=[pl.BlockSpec(memory_space=pltpu.SMEM), vmem, vmem, vmem],
        out_specs=vmem,
        out_shape=jax.ShapeDtypeStruct((HEADS, normed.shape[0], HEAD), BF),
        compiler_params=params(),
        name="query",
    )(slots, normed, mine, other)


def attend_kernel(scale, user_ref, query_ref, cache_ref, out_ref):
    sources, rows, _ = out_ref.shape

    def step(t, carry):
        users = [user_ref[s, t] for s in range(sources)]
        here = pl.ds(pl.multiple_of(t * TILE, TILE), TILE)
        weights = []
        for s, u in enumerate(users):
            turned = jnp.concatenate(
                [cache_ref[u, b : b + BLK, :] for b in range(0, HIST, BLK)], axis=1
            )
            score = jnp.dot(query_ref[s, here, :], turned, preferred_element_type=F32)
            weights.append(half_silu(score * (0.5 * scale)).astype(BF))
        for s, u in enumerate(users):
            out_ref[s, here, :] = jnp.dot(
                weights[s], cache_ref[u, HIST : 2 * HIST, :], preferred_element_type=F32
            ).astype(BF)
        return carry

    lax.fori_loop(0, rows // TILE, step, 0, unroll=4)


def attend(users, queries, caches, scale):
    vmem = pl.BlockSpec(memory_space=pltpu.VMEM)
    smem = pl.BlockSpec(memory_space=pltpu.SMEM)
    return pl.pallas_call(
        functools.partial(attend_kernel, scale),
        in_specs=[smem, vmem, vmem],
        out_specs=vmem,
        out_shape=jax.ShapeDtypeStruct(queries.shape, BF),
        compiler_params=params(),
        name="attend",
    )(users, queries, caches)


def own_kernel(scale, rows_ref, query_ref, key_w, value_w, gate_w, own_ref, gate_ref):
    rows = rows_ref[...]
    width = rows.shape[1]

    def project(weights):
        block = weights[...].reshape(2 * HEAD, width)
        made = lax.dot_general(rows, block, NT, preferred_element_type=F32)
        return half_silu(made * 0.5).astype(BF)

    self_keys = project(key_w).astype(F32)
    self_values = project(value_w).astype(F32)
    gate_ref[...] = project(gate_w)
    for lane in range(2):
        cut = slice(lane * HEAD, (lane + 1) * HEAD)
        products = query_ref[lane].astype(F32) * self_keys[:, cut]
        strength = half_silu(jnp.sum(products, axis=1, keepdims=True) * (0.5 * scale))
        own_ref[:, cut] = strength * self_values[:, cut]


def own(normed, queries, gathered, scale):
    total, width = normed.shape
    steps = width // (2 * HEAD)

    def weights(place):
        return pl.BlockSpec((2, HEAD, width), lambda i: (place * steps + i, 0, 0))

    return pl.pallas_call(
        functools.partial(own_kernel, scale),
        grid=(steps,),
        in_specs=[
            pl.BlockSpec((total, width), lambda i: (0, 0)),
            pl.BlockSpec((2, total, HEAD), lambda i: (i, 0, 0)),
            weights(1),
            weights(2),
            weights(3),
        ],
        out_specs=[pl.BlockSpec((total, 2 * HEAD), lambda i: (0, i))] * 2,
        out_shape=[
            jax.ShapeDtypeStruct((total, width), F32),
            jax.ShapeDtypeStruct((total, width), BF),
        ],
        compiler_params=params(56),
        name="own",
    )(normed, queries, gathered, gathered, gathered)


def turn_kernel(gathered, out_ref):
    shares, rows, _ = gathered.shape
    span = rows // NX
    for i in range(shares):
        for k in range(NX):
            first = (k * shares + i) * span
            out_ref[first : first + span, :] = gathered[i, k * span : (k + 1) * span, :]


def turn(gathered):
    rows, width = gathered.shape[1:]
    return pl.pallas_call(
        turn_kernel,
        grid=(1,),
        in_specs=[pl.BlockSpec((HEADS, rows, width), lambda i: (0, 0, 0))],
        out_specs=pl.BlockSpec((width, width), lambda i: (0, 0)),
        out_shape=jax.ShapeDtypeStruct((width, width), BF),
        compiler_params=params(56),
        name="turn",
    )(gathered)


def finish_kernel(count_ref, hist_ref, own_ref, gate_ref, out_w, rows_ref, out_ref):
    rows, width = rows_ref.shape
    history = jnp.concatenate([hist_ref[h].astype(F32) for h in range(HEADS)], axis=1)
    combined = history + own_ref[...]
    centred = combined - jnp.mean(combined, axis=-1, keepdims=True)
    variance = jnp.mean(centred * centred, axis=-1, keepdims=True)
    gated = centred * lax.rsqrt(variance + 1e-05) * gate_ref[...].astype(F32)
    mixed = jnp.dot(gated.astype(BF), out_w[...], preferred_element_type=F32)
    mixed = mixed + rows_ref[...].astype(F32)
    slot = lax.broadcasted_iota(jnp.int32, (TILE, width), 0)
    tile = pl.program_id(0) * (rows // TILE)
    for t in range(rows // TILE):
        cut = slice(t * TILE, (t + 1) * TILE)
        scored = jnp.where(slot < count_ref[tile + t], mixed[cut, :], 0.0)
        out_ref[cut, :] = scored.astype(BF)


def finish(counts, history, own_part, gate, out_w, candidates):
    total, width = candidates.shape
    place = pl.BlockSpec((PIECE, width), lambda i: (i, 0))
    return pl.pallas_call(
        finish_kernel,
        grid=(total // PIECE,),
        in_specs=[
            pl.BlockSpec(memory_space=pltpu.SMEM),
            pl.BlockSpec((HEADS, PIECE, HEAD), lambda i: (0, i, 0)),
            place,
            place,
            pl.BlockSpec((width, width), lambda i: (0, 0)),
            place,
        ],
        out_specs=place,
        out_shape=jax.ShapeDtypeStruct((total, width), BF),
        compiler_params=params(56),
        name="finish",
    )(counts, history, own_part, gate, out_w, candidates)


def swap_z(values):
    return lax.all_to_all(values, "z", split_axis=0, concat_axis=0, tiled=True)


def spread_y(part):
    up = lax.ppermute(part, "y", ring(NY, 1))
    down = lax.ppermute(part, "y", ring(NY, NY - 1))
    half = part.shape[0] // 2
    far = [
        lax.ppermute(up[:half], "y", ring(NY, 1)),
        lax.ppermute(down[half:], "y", ring(NY, NY - 1)),
    ]
    return jnp.concatenate([part, up] + far + [down], axis=0)


def shards(candidates, hist_kv, hist_len, block_mask, tile_user, tile_count, weight_in, weight_out):
    width = candidates.shape[1]
    tiles = tile_user.shape[0]
    scale = HEAD ** (-0.5)
    at_x, at_core, at_y, at_z = [lax.axis_index(name) for name in ("x", "core", "y", "z")]

    columns = weight_in.T
    share, out_share = columns.shape[0], weight_out.shape[0]
    normed = norm(candidates)
    both = jnp.concatenate([columns, weight_out], axis=0)
    meta = jnp.zeros((META, HEAD), BF).at[0, :tiles].set(tile_user[:, 0].astype(BF))
    caches = prep(hist_kv[0], hist_len, block_mask, meta)
    spread = [both] + [lax.ppermute(both, "z", ring(NZ, k)) for k in range(1, NZ)]
    caches, spread = lax.optimization_barrier((caches, spread))
    caches = swap_z(caches)
    spread = jnp.stack(spread)[(at_z - jnp.arange(NZ, dtype=jnp.int32)) % NZ]
    in_rows = spread[:, :share].reshape(NZ * share, width)
    out_rows = spread[:, share:].reshape(NZ * out_share, width)
    both = jnp.concatenate([in_rows, out_rows], axis=0)
    cut = in_rows.shape[0]
    sent = [lax.ppermute(both, "x", [(0, k), (k, 0)]) for k in range(1, NX)]
    query_z = jnp.where(at_x == 0, in_rows, sent[0][:cut] + sent[1][:cut] + sent[2][:cut])
    out_rows = jnp.concatenate([out_rows] + [piece[cut:] for piece in sent], axis=0)
    rest = jnp.where(at_x == 0, out_rows, in_rows)

    parts = [query_z] + [lax.ppermute(query_z, "y", ring(NY, k)) for k in range(1, NY)]
    parts, caches, normed = lax.optimization_barrier((parts, caches, normed))
    users = caches[:, 2 * HIST, :tiles].astype(jnp.int32)
    caches = lax.all_gather(caches, "y", axis=0, tiled=True)
    mine = jnp.concatenate(parts, axis=0)
    other = lax.ppermute(mine, "core", ring(NC, 1))
    at = (at_y - jnp.arange(NY, dtype=jnp.int32)) % NY
    slots = jnp.concatenate([at_core * NY + at, (1 - at_core) * NY + at]).astype(jnp.int32)

    queries = query(slots, normed, mine, other)
    rest, queries = lax.optimization_barrier((rest, queries))
    arrived = swap_z(queries)
    gathered = lax.all_gather(rest, ("x", "core", "y"))

    history = swap_z(attend(users, arrived, caches, scale))
    out_w = turn(gathered)
    own_part, gate = own(normed, queries, gathered, scale)
    return finish(tile_count, history, own_part, gate, out_w, candidates)


def solution(mesh):
    fine = Mesh(mesh.devices.reshape(NX, NC, NY, NZ), ("x", "core", "y", "z"))
    every = ("x", "core", "y", "z")
    in_specs = (
        P(every, None),
        P(every, None, None),
        P(every),
        P(every, None),
        P(every, None),
        P(every),
        P(None, every),
        P(every, None),
    )
    return jax.shard_map(
        shards, mesh=fine, in_specs=in_specs, out_specs=P(every, None), check_vma=False
    )
```
